256 devices in a mesh: ctx: 64 (over z, x_hi, y), head: 4 (over x_lo, core).
Axes of the slice: x: 4 (x_hi: 2, x_lo: 2; x = x_hi * 2 + x_lo), y: 4, z: 8, core: 2. Of those that a mesh axis runs over, the one named last changes fastest.
Arguments:
- ctx_query: bfloat16 [32768, 8192], P('ctx', 'head'), may hold values from -300 to 300
- ctx_key: bfloat16 [32768, 1024], P('ctx', 'head'), may hold values from -10 to 10
- ctx_value: bfloat16 [32768, 1024], P('ctx', 'head'), may hold values from -6 to 6
- valid: int32 [64], P('ctx'), may hold values from 1 to 512, as said below
- query_rows: bfloat16 [256, 8192], P(('ctx', 'head')), may hold values from -300 to 300
- offsets: int32 [256], P(('ctx', 'head')), may hold values from 512 to 32768, as said below
Outputs:
- block_out: bfloat16 [32768, 8192], P('ctx', 'head')
- query_out: bfloat16 [256, 8192], P(('ctx', 'head'))
The draws below stay inside these ranges and needn't reach their ends.
Inputs may be any that keep to these rules, and one draw needn't show every extreme that they name: Every block but the last holds 512 valid tokens. `offsets`: some row sees all 32768 context positions and some row only the first block.
All inputs are finite; a program needn't handle non-finite values.
Results may differ from the reference program's by a relative error of at most 0.0045.
Values may be sent and summed in bfloat16 or wider, within the bound.
No kernel may reach another device: no remote copies, remote signals or barrier semaphores. Data moves between devices by JAX's collectives and lax.ppermute only.
A program may use at most 64 MiB of HBM per device.

```python
import math
import jax
import jax.numpy as jnp
from jax import lax

QHEADS = 64
KVHEADS = 8
DH = 128
BLK = 512
BLOCKS = 64
TOKENS = 32768
QROWS = 256


def shared_keys(key):
    return jnp.clip(jax.random.normal(key, (TOKENS, KVHEADS * DH), jnp.float32), -4.5, 4.5)


def draw_ctx_key(key, part):
    base = shared_keys(key)
    return base.astype(jnp.bfloat16)


def draw_ctx_query(key, part):
    own_key = jax.random.fold_in(key, 5)
    values_drawn = jnp.clip(jax.random.normal(own_key, (TOKENS, QHEADS * DH), jnp.float32), -4.5, 4.5)
    return values_drawn.astype(jnp.bfloat16)


def draw_query_rows(key, part):
    own_key = jax.random.fold_in(key, 7)
    values_drawn = jnp.clip(jax.random.normal(own_key, (QROWS, QHEADS * DH), jnp.float32), -4.5, 4.5)
    return values_drawn.astype(jnp.bfloat16)


def draw_valid(key, part):
    own_key = jax.random.fold_in(key, 13)
    last_count = jax.random.randint(own_key, (), 1, BLK + 1, jnp.int32)
    return jnp.full((BLOCKS,), BLK, jnp.int32).at[BLOCKS - 1].set(last_count)


def draw_offsets(key, part):
    own_key = jax.random.fold_in(key, 14)
    drawn = jax.random.randint(own_key, (QROWS,), BLK, TOKENS + 1, jnp.int32)
    order = jax.random.permutation(jax.random.fold_in(own_key, 1), QROWS)
    drawn = drawn.at[order[0]].set(TOKENS)
    drawn = drawn.at[order[1]].set(BLK)
    return drawn


def block_scale(key, dims, split, low, top_value):
    loudness, own = 1.0, jax.random.fold_in(key, 6)
    for axis_at, blocks in split:
        draws = jnp.exp(jax.random.uniform(jax.random.fold_in(own, axis_at), (blocks,), jnp.float32, low / len(split), top_value / len(split)))
        loudness = loudness * jnp.repeat(draws, dims[axis_at] // blocks).reshape([-1 if axis == axis_at else 1 for axis in range(len(dims))])
    return loudness


def bell_draw(rng, shape, width, limit, shards=(), held_as=jnp.bfloat16):
    array = width * jax.random.normal(rng, shape, jnp.float32)
    if shards:
        array = array * block_scale(rng, shape, shards, -0.22, 0.18)
    return jnp.clip(array, -limit, limit).astype(held_as)


def setup_inputs(seed: int = 0) -> dict:
    splits = jax.random.split(jax.random.key(seed), 7)
    ctx_query = draw_ctx_query(jax.random.fold_in(splits[6], 71), 0)
    ctx_key = draw_ctx_key(jax.random.fold_in(splits[6], 71), 0)
    ctx_value = bell_draw(splits[2], (TOKENS, KVHEADS * DH), 1.0, 6.0, ((0, 64), (1, 4)))
    valid = draw_valid(jax.random.fold_in(splits[6], 71), 0)
    query_rows = draw_query_rows(jax.random.fold_in(splits[6], 71), 0)
    offsets = draw_offsets(jax.random.fold_in(splits[6], 71), 0)
    return {"ctx_query": ctx_query, "ctx_key": ctx_key, "ctx_value": ctx_value, "valid": valid, "query_rows": query_rows, "offsets": offsets}


def block_terms(queries, key_block, value_block, visible):
    scores = jnp.einsum('rhgd,shd->hgrs', queries.astype(jnp.float32), key_block.astype(jnp.float32)) * (1.0 / math.sqrt(DH))
    highest = lax.optimization_barrier(jnp.max(jnp.where(visible, scores, -1e+30), axis=-1))
    weights = jnp.where(visible, jnp.exp(scores - highest[..., None]), 0.0)
    totals = lax.optimization_barrier(jnp.sum(weights, axis=-1))
    rounded = lax.optimization_barrier(weights.astype(jnp.bfloat16))
    summed = jnp.einsum('hgrs,shd->rhgd', rounded.astype(jnp.float32), value_block.astype(jnp.float32))
    return (highest, totals, summed)

def reference(ctx_query, ctx_key, ctx_value, valid, query_rows, offsets):
    group_size = QHEADS // KVHEADS
    blocked_query = ctx_query.reshape(BLOCKS, BLK, KVHEADS, group_size, DH)
    blocked_key = ctx_key.reshape(BLOCKS, BLK, KVHEADS, DH)
    blocked_value = ctx_value.reshape(BLOCKS, BLK, KVHEADS, DH)
    row_ids = jnp.arange(BLK, dtype=jnp.int32)

    def phase_one(block_index):
        key_rows = jnp.concatenate([blocked_key[0], blocked_key[block_index]], axis=0)
        value_rows = jnp.concatenate([blocked_value[0], blocked_value[block_index]], axis=0)
        own_keys = (row_ids[None, :] <= row_ids[:, None]) & (row_ids[None, :] < valid[block_index])
        anchor_seen = jnp.broadcast_to(block_index > 0, (BLK, BLK))
        visible = jnp.concatenate([anchor_seen, own_keys], axis=1)
        highest, totals, summed = block_terms(blocked_query[block_index], key_rows, value_rows, visible)
        normed = summed / jnp.transpose(totals, (2, 0, 1))[..., None]
        return normed.astype(jnp.bfloat16).reshape(BLK, QHEADS * DH)
    block_out = lax.map(phase_one, jnp.arange(BLOCKS, dtype=jnp.int32)).reshape(TOKENS, QHEADS * DH)
    grouped_rows = query_rows.reshape(QROWS, KVHEADS, group_size, DH)

    def phase_two(block_index):
        positions = block_index * BLK + row_ids
        visible = (row_ids[None, :] < valid[block_index]) & (positions[None, :] < offsets[:, None])
        return block_terms(grouped_rows, blocked_key[block_index], blocked_value[block_index], visible)
    highest, totals, summed = lax.map(phase_two, jnp.arange(BLOCKS, dtype=jnp.int32))
    overall = lax.optimization_barrier(jnp.max(highest, axis=0))
    factor = jnp.exp(highest - overall[None])
    numerator = jnp.einsum('bhgr,brhgd->rhgd', factor, summed, precision=lax.Precision.HIGHEST)
    denominator = lax.optimization_barrier(jnp.sum(factor * totals, axis=0))
    merged = numerator / jnp.transpose(denominator, (2, 0, 1))[..., None]
    query_out = merged.astype(jnp.bfloat16).reshape(QROWS, QHEADS * DH)
    return (block_out, query_out)
```

```python
import functools
import math

import jax
import jax.numpy as jnp
from jax import lax
from jax.experimental import pallas as pl
from jax.experimental.pallas import tpu as pltpu
from jax.sharding import Mesh, PartitionSpec as P

DH = 128
KV_HEADS_HERE = 2
GROUP = 8
BLK = 512
NZ, NXH, NY, NXL, NCORE = 8, 2, 4, 2, 2
PEERS = NZ * NXH * NXL * NCORE
ROWS = PEERS
QUARTER = BLK // NY
EXPONENT = math.log2(math.e) / math.sqrt(DH)
HIDDEN = -1e30
FLOOR = -1e29
CTX = ("z", "xh", "y")
ZX = ("z", "xh")
HEAD = ("xl", "core")
PLANE = ("z", "xh", "xl", "core")
BF16 = jnp.bfloat16
F32 = jnp.float32


def dot_keys(queries, keys):
    return lax.dot_general(queries, keys, (((1,), (1,)), ((), ())), preferred_element_type=F32)


def dot_values(probs, values):
    return jnp.dot(probs, values, preferred_element_type=F32)


def block_kernel(heads, chunk, stack, valid_ref, q_ref, k_ref, v_ref, a0, a1, a2, a3, o_ref, keys, values):
    @pl.when(pl.program_id(1) == 0)
    def _():
        valid = valid_ref[0]
        seen = (lax.axis_index("z") + lax.axis_index("xh") + lax.axis_index("y")) > 0
        keep = lax.broadcasted_iota(jnp.int32, (BLK, DH), 0) < valid
        base = k_ref[0:1, :].astype(F32)
        keys[BLK:, :] = jnp.where(keep, k_ref[...].astype(F32), base).astype(BF16)
        values[BLK:, :DH] = jnp.where(keep, v_ref[...].astype(F32), 0.0).astype(BF16)
        values[BLK:, DH:] = jnp.where(keep, 1.0, 0.0).astype(BF16)
        for i, piece in enumerate((a0, a1, a2, a3)):
            rows = slice(QUARTER * i, QUARTER * (i + 1))
            keys[rows, :] = jnp.where(seen, piece[0:QUARTER, :].astype(F32), base).astype(BF16)
            values[rows, :DH] = jnp.where(seen, piece[QUARTER:, :].astype(F32), 0.0).astype(BF16)
        values[0:BLK, DH:] = jnp.where(seen, jnp.ones((BLK, DH), F32), 0.0).astype(BF16)

    rows = stack * chunk
    row = lax.broadcasted_iota(jnp.int32, (rows, chunk), 0) & (chunk - 1)
    causal = lax.broadcasted_iota(jnp.int32, (rows, chunk), 1) <= row
    items = [(h, r) for h in range(0, heads, stack) for r in range(BLK // chunk)]

    def scores(h, r):
        q = [q_ref[r * chunk : (r + 1) * chunk, (h + i) * DH : (h + i + 1) * DH] for i in range(stack)]
        q = q[0] if stack == 1 else jnp.concatenate(q, axis=0)
        return dot_keys(q, keys[0 : BLK + (r + 1) * chunk, :])

    def finish(h, r, s):
        n = BLK + r * chunk
        tail = jnp.where(causal, s[:, n:], HIDDEN)
        full = s[:, :n]
        top = jnp.maximum(jnp.max(full, axis=1, keepdims=True), jnp.max(tail, axis=1, keepdims=True))
        probs = jnp.concatenate(
            [jnp.exp2((full - top) * EXPONENT).astype(BF16), jnp.exp2((tail - top) * EXPONENT).astype(BF16)], axis=1
        )
        acc = dot_values(probs, values[0 : n + chunk, :])
        out = (acc[:, :DH] / acc[:, DH:]).astype(BF16)
        for i in range(stack):
            o_ref[r * chunk : (r + 1) * chunk, (h + i) * DH : (h + i + 1) * DH] = out[i * chunk : (i + 1) * chunk]

    s = scores(*items[0])
    for n, item in enumerate(items):
        following = scores(*items[n + 1]) if n + 1 < len(items) else None
        finish(*item, s)
        s = following


def block_attention(valid, q, k, v, pieces, heads=8, chunk=128, stack=2):
    steps = GROUP // heads
    kv = pl.BlockSpec((BLK, DH), lambda g, i: (0, g))
    piece = pl.BlockSpec((2 * QUARTER, DH), lambda g, i: (0, g))
    q_spec = pl.BlockSpec((BLK, heads * DH), lambda g, i: (0, g * steps + i))
    return pl.pallas_call(
        functools.partial(block_kernel, heads, chunk, stack),
        grid=(KV_HEADS_HERE, steps),
        in_specs=[pl.BlockSpec(memory_space=pltpu.SMEM), q_spec, kv, kv, piece, piece, piece, piece],
        out_specs=q_spec,
        scratch_shapes=[pltpu.VMEM((2 * BLK, DH), BF16), pltpu.VMEM((2 * BLK, 2 * DH), BF16)],
        out_shape=jax.ShapeDtypeStruct(q.shape, BF16),
        compiler_params=pltpu.CompilerParams(vmem_limit_bytes=40 << 20),
        cost_estimate=pl.CostEstimate(flops=4_000_000_000, bytes_accessed=5 << 20, transcendentals=7 << 20),
        name="block_attention",
    )(valid, q, k, v, *pieces)


def rows_kernel(chunk, valid_ref, msg_ref, k_ref, v_ref, m1, m2, m3, o_ref, keys, values):
    my_y = lax.axis_index("y")
    first = (lax.axis_index("z") * NXH + lax.axis_index("xh")) * NY
    valids, bases = [valid_ref[0].astype(F32)], [(first + my_y) * BLK]
    for message, step in ((m1, 3), (m2, 1), (m3, 2)):
        digits = message[2 * BLK :, :].astype(F32)
        valids.append(digits[0:1, 0:1] * 256.0 + digits[0:1, DH : DH + 1])
        bases.append((first + lax.rem(my_y + step, NY)) * BLK)
    arrived = msg_ref[...].astype(F32)
    limits_in = arrived[:, 16:24, :].reshape(ROWS * GROUP, DH)
    offsets = limits_in[:, 0:1] * 256.0 + limits_in[:, 64:65]
    limits = [jnp.minimum(offsets - base.astype(F32), v) for base, v in zip(bases, valids)]
    columns = lax.broadcasted_iota(jnp.int32, (chunk, BLK), 1).astype(F32)
    values[:, DH:] = jnp.ones((NY * BLK, DH), BF16)
    outs, sums = [], []
    for g in range(KV_HEADS_HERE):
        lanes = slice(g * DH, (g + 1) * DH)
        keys[0:BLK, :] = k_ref[:, lanes]
        values[0:BLK, :DH] = v_ref[:, lanes]
        for i, message in enumerate((m1, m2, m3)):
            rows = slice((i + 1) * BLK, (i + 2) * BLK)
            keys[rows, :] = message[0:BLK, lanes]
            values[rows, :DH] = message[BLK : 2 * BLK, lanes]
        queries = arrived[:, 8 * g : 8 * g + 8, :].reshape(ROWS * GROUP, DH).astype(BF16)
        parts, logs = [], []
        for r in range(0, ROWS * GROUP, chunk):
            s = dot_keys(queries[r : r + chunk], keys[...])
            pieces = [
                jnp.where(columns < limits[b][r : r + chunk], s[:, b * BLK : (b + 1) * BLK], HIDDEN) for b in range(NY)
            ]
            top = jnp.max(functools.reduce(jnp.maximum, pieces), axis=1, keepdims=True)
            top = jnp.maximum(top, FLOOR)
            probs = jnp.concatenate([jnp.exp2((p - top) * EXPONENT).astype(BF16) for p in pieces], axis=1)
            acc = dot_values(probs, values[...])
            total = acc[:, DH:]
            some = total > 0.0
            parts.append(acc[:, :DH] / jnp.where(some, total, 1.0))
            logs.append(jnp.where(some, top * EXPONENT + jnp.log2(jnp.where(some, total, 1.0)), HIDDEN))
        outs.append(jnp.concatenate(parts, axis=0).reshape(ROWS, GROUP, DH))
        sums.append(jnp.concatenate(logs, axis=0))
    lane = lax.broadcasted_iota(jnp.int32, (ROWS * GROUP, DH), 1)
    log = jnp.where(lane < 64, sums[0], sums[1])
    high = log.astype(BF16).astype(F32)
    middle = (log - high).astype(BF16).astype(F32)
    low = log - high - middle
    lane = lane & 63
    log = jnp.where(lane == 0, high, jnp.where(lane == 1, middle, low)).reshape(ROWS, GROUP, DH)
    o_ref[...] = jnp.concatenate(outs + [log], axis=1).astype(BF16)


def rows_attention(valid, msg, k, v, others, chunk=128):
    whole = pl.BlockSpec(memory_space=pltpu.VMEM)
    return pl.pallas_call(
        functools.partial(rows_kernel, chunk),
        in_specs=[pl.BlockSpec(memory_space=pltpu.SMEM)] + [whole] * 6,
        out_specs=whole,
        scratch_shapes=[pltpu.VMEM((NY * BLK, DH), BF16), pltpu.VMEM((NY * BLK, 2 * DH), BF16)],
        out_shape=jax.ShapeDtypeStruct(msg.shape, BF16),
        compiler_params=pltpu.CompilerParams(vmem_limit_bytes=40 << 20),
        cost_estimate=pl.CostEstimate(flops=1_100_000_000, bytes_accessed=3 << 20, transcendentals=2 << 20),
        name="rows_attention",
    )(valid, msg, k, v, *others)


def merge_kernel(msg_ref, o_ref):
    arrived = msg_ref[...].astype(F32).reshape(NZ * NXH, NXL * NCORE, 24, DH)
    for h in range(NXL * NCORE):
        for g in range(KV_HEADS_HERE):
            digits = arrived[:, h, 16:24, :]
            at = 64 * g
            log = digits[:, :, at : at + 1] + digits[:, :, at + 1 : at + 2] + digits[:, :, at + 2 : at + 3]
            factor = jnp.exp2(log - jnp.max(log, axis=0, keepdims=True))
            total = jnp.sum(factor, axis=0)
            merged = jnp.sum(factor * arrived[:, h, 8 * g : 8 * g + 8, :], axis=0) / total
            start = (h * KV_HEADS_HERE + g) * GROUP
            o_ref[start : start + GROUP, :] = merged


def merge(msg):
    whole = pl.BlockSpec(memory_space=pltpu.VMEM)
    return pl.pallas_call(
        merge_kernel,
        in_specs=[whole],
        out_specs=whole,
        out_shape=jax.ShapeDtypeStruct((NXL * NCORE * KV_HEADS_HERE * GROUP, DH), F32),
        name="merge",
    )(msg)


def shift(n, by):
    return [(i, (i + by) % n) for i in range(n)]


def digits_of(number):
    high = number // 256
    return high.astype(BF16), (number - high * 256).astype(BF16)


def place(z, xh):
    return (z % NZ) * NXH + xh


def to_ring(array):
    return [lax.ppermute(array, "y", shift(NY, by)) for by in (1, -1, 2)]


def spread_anchor(kv):
    quarters = [jnp.concatenate([kv[r : r + QUARTER], kv[BLK + r : BLK + r + QUARTER]]) for r in range(0, BLK, QUARTER)]
    current = jnp.where(lax.axis_index(CTX) == 0, quarters[0], jnp.zeros_like(quarters[0]))
    for y in range(1, NY):
        current = current + lax.ppermute(quarters[y], CTX, [(0, y)])
    sent = [lax.ppermute(current, ZX, [(0, place(z, 0))]) for z in (2, 4, 6)]
    current = current + sent[0] + sent[1] + sent[2]
    even = (0, 2, 4, 6)
    sent = [
        lax.ppermute(current, ZX, [(place(z, 0), place(z + dz, xh)) for z in even]) for dz, xh in ((0, 1), (1, 0), (1, 1))
    ]
    current = current + sent[0] + sent[1] + sent[2]
    return [current] + to_ring(current)


def on_device(ctx_query, ctx_key, ctx_value, valid, query_rows, offsets):
    high, low = digits_of(valid)
    extra = jnp.concatenate([jnp.broadcast_to(high[None], (16, DH)), jnp.broadcast_to(low[None], (16, DH))], axis=1)
    kv = jnp.concatenate([ctx_key, ctx_value, extra], axis=0)
    others = to_ring(kv)

    high, low = digits_of(offsets)
    limit = jnp.concatenate(
        [jnp.broadcast_to(high[None, None], (4, 8, 64)), jnp.broadcast_to(low[None, None], (4, 8, 64))], axis=2
    )
    message = jnp.concatenate([query_rows.reshape(4, 16, DH), limit], axis=1)
    message = jnp.broadcast_to(message[None], (NZ * NXH, 4, 24, DH)).reshape(PEERS, 24, DH)
    message = lax.all_to_all(message, PLANE, 0, 0, tiled=True)

    pieces = spread_anchor(kv)
    partial = rows_attention(valid, message, ctx_key, ctx_value, others)
    partial = lax.all_to_all(partial, PLANE, 0, 0, tiled=True)
    block_out = block_attention(valid, ctx_query, ctx_key, ctx_value, pieces)
    query_out = merge(partial).astype(BF16).reshape(1, -1)
    return (block_out, query_out)


def solution(mesh):
    fine = Mesh(mesh.devices.reshape(NZ, NXH, NY, NXL, NCORE), ("z", "xh", "y", "xl", "core"))
    return jax.shard_map(
        on_device,
        mesh=fine,
        in_specs=(P(CTX, HEAD), P(CTX, HEAD), P(CTX, HEAD), P(CTX), P(CTX + HEAD, None), P(CTX + HEAD)),
        out_specs=(P(CTX, HEAD), P(CTX + HEAD, None)),
        check_vma=False,
    )
```

```python
import functools
import math

import jax
import jax.numpy as jnp
from jax import lax
from jax.experimental import pallas as pl
from jax.experimental.pallas import tpu as pltpu
from jax.sharding import Mesh, PartitionSpec as P

DH = 128
KV_HEADS_HERE = 2
GROUP = 8
BLK = 512
NZ, NXH, NY, NXL, NCORE = 8, 2, 4, 2, 2
PEERS = NZ * NXH * NXL * NCORE
ROWS = PEERS
QUARTER = BLK // NY
EXPONENT = math.log2(math.e) / math.sqrt(DH)
HIDDEN = -1e30
FLOOR = -1e29
CTX = ("z", "xh", "y")
ZX = ("z", "xh")
HEAD = ("xl", "core")
PLANE = ("z", "xh", "xl", "core")
BF16 = jnp.bfloat16
F32 = jnp.float32


SMALL = pltpu.CompilerParams(vmem_limit_bytes=6 << 20)
LONG = pl.CostEstimate(flops=10**12, bytes_accessed=1 << 20, transcendentals=0)


def dot_keys(queries, keys):
    return lax.dot_general(queries, keys, (((1,), (1,)), ((), ())), preferred_element_type=F32)


def dot_values(probs, values):
    return jnp.dot(probs, values, preferred_element_type=F32)


def block_kernel(heads, chunk, stack, valid_ref, q_ref, k_ref, v_ref, a0, a1, a2, a3, o_ref, keys, values):
    @pl.when(pl.program_id(1) == 0)
    def _():
        valid = valid_ref[0]
        seen = (lax.axis_index("z") + lax.axis_index("xh") + lax.axis_index("y")) > 0
        keep = lax.broadcasted_iota(jnp.int32, (BLK, DH), 0) < valid
        base = k_ref[0:1, :].astype(F32)
        keys[BLK:, :] = jnp.where(keep, k_ref[...].astype(F32), base).astype(BF16)
        values[BLK:, :DH] = jnp.where(keep, v_ref[...].astype(F32), 0.0).astype(BF16)
        values[BLK:, DH:] = jnp.where(keep, 1.0, 0.0).astype(BF16)
        for i, piece in enumerate((a0, a1, a2, a3)):
            rows = slice(QUARTER * i, QUARTER * (i + 1))
            keys[rows, :] = jnp.where(seen, piece[0:QUARTER, :].astype(F32), base).astype(BF16)
            values[rows, :DH] = jnp.where(seen, piece[QUARTER:, :].astype(F32), 0.0).astype(BF16)
        values[0:BLK, DH:] = jnp.where(seen, jnp.ones((BLK, DH), F32), 0.0).astype(BF16)

    rows = stack * chunk
    row = lax.broadcasted_iota(jnp.int32, (rows, chunk), 0) & (chunk - 1)
    causal = lax.broadcasted_iota(jnp.int32, (rows, chunk), 1) <= row
    items = [(h, r) for h in range(0, heads, stack) for r in range(BLK // chunk)]

    def scores(h, r):
        q = [q_ref[r * chunk : (r + 1) * chunk, (h + i) * DH : (h + i + 1) * DH] for i in range(stack)]
        q = q[0] if stack == 1 else jnp.concatenate(q, axis=0)
        return dot_keys(q, keys[0 : BLK + (r + 1) * chunk, :])

    def finish(h, r, s):
        n = BLK + r * chunk
        tail = jnp.where(causal, s[:, n:], HIDDEN)
        full = s[:, :n]
        top = jnp.maximum(jnp.max(full, axis=1, keepdims=True), jnp.max(tail, axis=1, keepdims=True))
        probs = jnp.concatenate(
            [jnp.exp2((full - top) * EXPONENT).astype(BF16), jnp.exp2((tail - top) * EXPONENT).astype(BF16)], axis=1
        )
        acc = dot_values(probs, values[0 : n + chunk, :])
        out = (acc[:, :DH] / acc[:, DH:]).astype(BF16)
        for i in range(stack):
            o_ref[r * chunk : (r + 1) * chunk, (h + i) * DH : (h + i + 1) * DH] = out[i * chunk : (i + 1) * chunk]

    s = scores(*items[0])
    for n, item in enumerate(items):
        following = scores(*items[n + 1]) if n + 1 < len(items) else None
        finish(*item, s)
        s = following


def block_attention(valid, q, k, v, pieces, heads=8, chunk=128, stack=2):
    steps = GROUP // heads
    kv = pl.BlockSpec((BLK, DH), lambda g, i: (0, g))
    piece = pl.BlockSpec((2 * QUARTER, DH), lambda g, i: (0, g))
    q_spec = pl.BlockSpec((BLK, heads * DH), lambda g, i: (0, g * steps + i))
    return pl.pallas_call(
        functools.partial(block_kernel, heads, chunk, stack),
        grid=(KV_HEADS_HERE, steps),
        in_specs=[pl.BlockSpec(memory_space=pltpu.SMEM), q_spec, kv, kv, piece, piece, piece, piece],
        out_specs=q_spec,
        scratch_shapes=[pltpu.VMEM((2 * BLK, DH), BF16), pltpu.VMEM((2 * BLK, 2 * DH), BF16)],
        out_shape=jax.ShapeDtypeStruct(q.shape, BF16),
        compiler_params=pltpu.CompilerParams(vmem_limit_bytes=20 << 20),
        cost_estimate=pl.CostEstimate(flops=12_000_000_000, bytes_accessed=5 << 20, transcendentals=7 << 20),
        name="block_attention",
    )(valid, q, k, v, *pieces)


def rows_kernel(chunk, valid_ref, msg_ref, k_ref, v_ref, m1, m2, k3, v3, *rest):
    o_ref, keys, values, sent = rest[-4:]
    g = pl.program_id(0)
    my_y = lax.axis_index("y")
    first = (lax.axis_index("z") * NXH + lax.axis_index("xh")) * NY
    valids, bases = [valid_ref[0].astype(F32)], [(first + my_y) * BLK]
    for message, step in ((m1, 3), (m2, 1), (k3, 2)):
        digits = message[BLK : BLK + 16, :].astype(F32)
        valids.append(digits[0:1, 0:1] * 256.0 + digits[8:9, 0:1])
        bases.append((first + lax.rem(my_y + step, NY)) * BLK)
    arrived = msg_ref[...].astype(F32)
    limits_in = arrived[:, 16:24, :].reshape(ROWS * GROUP, DH)
    offsets = limits_in[:, 0:1] * 256.0 + limits_in[:, 64:65]
    limits = [jnp.minimum(offsets - base.astype(F32), v) for base, v in zip(bases, valids)]
    columns = lax.broadcasted_iota(jnp.int32, (chunk, BLK), 1).astype(F32)
    keys[0:BLK, :] = k_ref[...]
    values[0:BLK, :DH] = v_ref[...]
    values[:, DH:] = jnp.ones((NY * BLK, DH), BF16)
    for i, message in enumerate((m1, m2)):
        rows = slice((i + 1) * BLK, (i + 2) * BLK)
        keys[rows, :] = message[0:BLK, :]
        values[rows, :DH] = message[BLK + 16 :, :]
    keys[3 * BLK :, :] = k3[0:BLK, :]
    values[3 * BLK :, :DH] = v3[...]
    queries = jnp.where(g == 0, arrived[:, :GROUP, :], arrived[:, GROUP : 2 * GROUP, :])
    queries = queries.reshape(ROWS * GROUP, DH).astype(BF16)
    starts = range(0, ROWS * GROUP, chunk)
    parts, logs = [], []
    s = dot_keys(queries[0:chunk], keys[...])
    for r in starts:
        following = dot_keys(queries[r + chunk : r + 2 * chunk], keys[...]) if r + chunk < ROWS * GROUP else None
        pieces = [
            jnp.where(columns < limits[b][r : r + chunk], s[:, b * BLK : (b + 1) * BLK], HIDDEN) for b in range(NY)
        ]
        top = jnp.max(functools.reduce(jnp.maximum, pieces), axis=1, keepdims=True)
        top = jnp.maximum(top, FLOOR)
        probs = jnp.concatenate([jnp.exp2((p - top) * EXPONENT).astype(BF16) for p in pieces], axis=1)
        acc = dot_values(probs, values[...])
        total = acc[:, DH:]
        some = total > 0.0
        parts.append(acc[:, :DH] / jnp.where(some, total, 1.0))
        logs.append(jnp.where(some, top * EXPONENT + jnp.log2(jnp.where(some, total, 1.0)), HIDDEN))
        s = following
    out = jnp.concatenate(parts, axis=0).reshape(ROWS, GROUP, DH)
    log = jnp.concatenate(logs, axis=0)
    lane = lax.broadcasted_iota(jnp.int32, (ROWS * GROUP, DH), 1) & 63
    high = log.astype(BF16).astype(F32)
    middle = (log - high).astype(BF16).astype(F32)
    low = log - high - middle
    log = jnp.where(lane == 0, high, jnp.where(lane == 1, middle, low)).reshape(ROWS, GROUP, DH)

    @pl.when(g == 0)
    def _():
        sent[:, 0:8, :] = out
        sent[:, 8:16, :] = log

    @pl.when(g == 1)
    def _():
        both = jnp.where(lane.reshape(ROWS, GROUP, DH) == lax.broadcasted_iota(jnp.int32, log.shape, 2), sent[:, 8:16, :], log)
        o_ref[...] = jnp.concatenate([sent[:, 0:8, :], out, both], axis=1).astype(BF16)


def rows_attention(valid, msg, k, v, others, after, chunk=128):
    whole = pl.BlockSpec(msg.shape, lambda g: (0, 0, 0))
    block = pl.BlockSpec((BLK, DH), lambda g: (0, g))
    other = [pl.BlockSpec((array.shape[0], DH), lambda g: (0, g)) for array in others]
    unread = [pl.BlockSpec(memory_space=pl.ANY)] * len(after)
    return pl.pallas_call(
        functools.partial(rows_kernel, chunk),
        grid=(KV_HEADS_HERE,),
        in_specs=[pl.BlockSpec(memory_space=pltpu.SMEM), whole, block, block, *other, *unread],
        out_specs=whole,
        scratch_shapes=[
            pltpu.VMEM((NY * BLK, DH), BF16),
            pltpu.VMEM((NY * BLK, 2 * DH), BF16),
            pltpu.VMEM((ROWS, 2 * GROUP, DH), F32),
        ],
        out_shape=jax.ShapeDtypeStruct(msg.shape, BF16),
        compiler_params=pltpu.CompilerParams(vmem_limit_bytes=20 << 20),
        cost_estimate=pl.CostEstimate(flops=7_000_000_000, bytes_accessed=3 << 20, transcendentals=2 << 20),
        name="rows_attention",
    )(valid, msg, k, v, *others, *after)


def merge_kernel(msg_ref, o_ref):
    arrived = msg_ref[...].astype(F32).reshape(NZ * NXH, NXL * NCORE, 24, DH)
    for h in range(NXL * NCORE):
        for g in range(KV_HEADS_HERE):
            digits = arrived[:, h, 16:24, :]
            at = 64 * g
            log = digits[:, :, at : at + 1] + digits[:, :, at + 1 : at + 2] + digits[:, :, at + 2 : at + 3]
            factor = jnp.exp2(log - jnp.max(log, axis=0, keepdims=True))
            total = jnp.sum(factor, axis=0)
            merged = jnp.sum(factor * arrived[:, h, 8 * g : 8 * g + 8, :], axis=0) / total
            for i in range(GROUP):
                at = ((h * KV_HEADS_HERE + g) * GROUP + i) * DH
                o_ref[0:1, at : at + DH] = merged[i : i + 1].astype(BF16)


def merge(msg):
    whole = pl.BlockSpec(memory_space=pltpu.VMEM)
    return pl.pallas_call(
        merge_kernel,
        in_specs=[whole],
        out_specs=whole,
        out_shape=jax.ShapeDtypeStruct((1, NXL * NCORE * KV_HEADS_HERE * GROUP * DH), BF16),
        compiler_params=pltpu.CompilerParams(vmem_limit_bytes=6 << 20),
        name="merge",
    )(msg)


def shift(n, by):
    return [(i, (i + by) % n) for i in range(n)]


def digits_of(number):
    high = number // 256
    return high.astype(BF16), (number - high * 256).astype(BF16)


def message_kernel(offset_ref, q_ref, _, o_ref, rows):
    offset = offset_ref[0]
    high, low = (offset >> 8).astype(F32), (offset & 255).astype(F32)
    lane = lax.broadcasted_iota(jnp.int32, (GROUP, DH), 1)
    limit = jnp.where(lane < 64, high, low)
    heads = KV_HEADS_HERE * GROUP
    for h in range(NXL * NCORE):
        for i in range(heads):
            at = (h * heads + i) * DH
            rows[h, i : i + 1, :] = q_ref[0:1, at : at + DH].astype(F32)
        rows[h, heads:, :] = limit
    o_ref[...] = jnp.broadcast_to(rows[...].astype(BF16)[None], o_ref.shape)


def row_message(offsets, query_rows, after):
    whole = pl.BlockSpec(memory_space=pltpu.VMEM)
    groups = NXL * NCORE
    out = pl.pallas_call(
        message_kernel,
        in_specs=[pl.BlockSpec(memory_space=pltpu.SMEM), whole, pl.BlockSpec(memory_space=pl.ANY)],
        out_specs=whole,
        scratch_shapes=[pltpu.VMEM((groups, 24, DH), F32)],
        out_shape=jax.ShapeDtypeStruct((NZ * NXH, groups, 24, DH), BF16),
        compiler_params=pltpu.CompilerParams(vmem_limit_bytes=6 << 20),
        cost_estimate=pl.CostEstimate(flops=10**12, bytes_accessed=1 << 20, transcendentals=0),
        name="row_message",
    )(offsets, query_rows, after)
    return out.reshape(PEERS, 24, DH)


def place(z, xh):
    return (z % NZ) * NXH + xh


def to_ring(array):
    return [lax.ppermute(array, "y", shift(NY, by)) for by in (1, -1, 2)]


def ring_blocks(kv):
    before, behind = lax.ppermute(kv, "y", shift(NY, 1)), lax.ppermute(kv, "y", shift(NY, -1))
    keys, values = halves(before, behind)
    far_keys = lax.ppermute(keys, "y", shift(NY, 1))
    far_values = lax.ppermute(values, "y", shift(NY, -1))
    return [before, behind, far_keys, far_values], keys


def anchor_quarters(k, v):
    quarters = [jnp.concatenate([k[r : r + QUARTER], v[r : r + QUARTER]]) for r in range(0, BLK, QUARTER)]
    current = jnp.where(lax.axis_index(CTX) == 0, quarters[0], jnp.zeros_like(quarters[0]))
    for y in range(1, NY):
        current = current + lax.ppermute(quarters[y], CTX, [(0, y)])
    return current


def anchor_tree(current, after):
    sent = [lax.ppermute(current, ZX, [(0, place(z, 0))]) for z in (2, 4, 6)]
    current = join([current] + sent, (after,))
    even = (0, 2, 4, 6)
    sent = [
        lax.ppermute(current, ZX, [(place(z, 0), place(z + dz, xh)) for z in even]) for dz, xh in ((0, 1), (1, 0), (1, 1))
    ]
    return current + sent[0] + sent[1] + sent[2]


def join_kernel(count, *refs):
    total = refs[0][...]
    for ref in refs[1:count]:
        total = total + ref[...]
    refs[-1][...] = total


def join(parts, after=()):
    whole = pl.BlockSpec(memory_space=pltpu.VMEM)
    return pl.pallas_call(
        functools.partial(join_kernel, len(parts)),
        in_specs=[whole] * len(parts) + [pl.BlockSpec(memory_space=pl.ANY)] * len(after),
        out_specs=whole,
        out_shape=jax.ShapeDtypeStruct(parts[0].shape, BF16),
        compiler_params=SMALL,
        cost_estimate=LONG,
        name="join",
    )(*parts, *after)


def halves_kernel(before, behind, keys, values):
    keys[...] = before[0 : BLK + 16, :]
    values[...] = behind[BLK + 16 :, :]


def halves(before, behind):
    whole = pl.BlockSpec(memory_space=pltpu.VMEM)
    return pl.pallas_call(
        halves_kernel,
        in_specs=[whole] * 2,
        out_specs=[whole] * 2,
        out_shape=[jax.ShapeDtypeStruct((rows, before.shape[1]), BF16) for rows in (BLK + 16, BLK)],
        compiler_params=SMALL,
        cost_estimate=LONG,
        name="halves",
    )(before, behind)


def on_device(ctx_query, ctx_key, ctx_value, valid, query_rows, offsets):
    high, low = digits_of(valid)
    extra = jnp.concatenate([jnp.broadcast_to(high[None], (8, 2 * DH)), jnp.broadcast_to(low[None], (8, 2 * DH))], axis=0)
    kv = jnp.concatenate([ctx_key, extra, ctx_value], axis=0)
    current = anchor_quarters(ctx_key, ctx_value)
    others, keys = ring_blocks(kv)
    message = row_message(offsets, query_rows, current)
    message = lax.all_to_all(message, PLANE, 0, 0, tiled=True)
    current = anchor_tree(current, keys)
    pieces = [current] + to_ring(current)
    partial = rows_attention(valid, message, ctx_key, ctx_value, others, [current])
    partial = lax.all_to_all(partial, PLANE, 0, 0, tiled=True)
    block_out = block_attention(valid, ctx_query, ctx_key, ctx_value, pieces)
    return (block_out, merge(partial))


def solution(mesh):
    fine = Mesh(mesh.devices.reshape(NZ, NXH, NY, NXL, NCORE), ("z", "xh", "y", "xl", "core"))
    return jax.shard_map(
        on_device,
        mesh=fine,
        in_specs=(P(CTX, HEAD), P(CTX, HEAD), P(CTX, HEAD), P(CTX), P(CTX + HEAD, None), P(CTX + HEAD)),
        out_specs=(P(CTX, HEAD), P(CTX + HEAD, None)),
        check_vma=False,
    )
```

```python
import functools
import math

import jax
import jax.numpy as jnp
from jax import lax
from jax.experimental import pallas as pl
from jax.experimental.pallas import tpu as pltpu
from jax.sharding import Mesh, PartitionSpec as P

DH = 128
KV_HEADS_HERE = 2
GROUP = 8
BLK = 512
NZ, NXH, NY, NXL, NCORE = 8, 2, 4, 2, 2
PEERS = NZ * NXH * NXL * NCORE
ROWS = PEERS
QUARTER = BLK // NY
EXPONENT = math.log2(math.e) / math.sqrt(DH)
HIDDEN = -1e30
FLOOR = -1e29
CTX = ("z", "xh", "y")
ZX = ("z", "xh")
HEAD = ("xl", "core")
PLANE = ("z", "xh", "xl", "core")
BF16 = jnp.bfloat16
F32 = jnp.float32


SMALL = pltpu.CompilerParams(vmem_limit_bytes=6 << 20)
LONG = pl.CostEstimate(flops=5 * 10**10, bytes_accessed=1 << 20, transcendentals=0)


def dot_keys(queries, keys):
    return lax.dot_general(queries, keys, (((1,), (1,)), ((), ())), preferred_element_type=F32)


def dot_values(probs, values):
    return jnp.dot(probs, values, preferred_element_type=F32)


def block_kernel(heads, chunk, stack, valid_ref, q_ref, k_ref, v_ref, a0, a1, a2, a3, o_ref, keys, values):
    @pl.when(pl.program_id(1) == 0)
    def _():
        valid = valid_ref[0]
        seen = (lax.axis_index("z") + lax.axis_index("xh") + lax.axis_index("y")) > 0
        keep = lax.broadcasted_iota(jnp.int32, (BLK, DH), 0) < valid
        base = k_ref[0:1, :].astype(F32)
        keys[BLK:, :] = jnp.where(keep, k_ref[...].astype(F32), base).astype(BF16)
        values[BLK:, :DH] = jnp.where(keep, v_ref[...].astype(F32), 0.0).astype(BF16)
        values[BLK:, DH:] = jnp.where(keep, 1.0, 0.0).astype(BF16)
        for i, piece in enumerate((a0, a1, a2, a3)):
            rows = slice(QUARTER * i, QUARTER * (i + 1))
            keys[rows, :] = jnp.where(seen, piece[0:QUARTER, :].astype(F32), base).astype(BF16)
            values[rows, :DH] = jnp.where(seen, piece[QUARTER:, :].astype(F32), 0.0).astype(BF16)
        values[0:BLK, DH:] = jnp.where(seen, jnp.ones((BLK, DH), F32), 0.0).astype(BF16)

    rows = stack * chunk
    row = lax.broadcasted_iota(jnp.int32, (rows, chunk), 0) & (chunk - 1)
    causal = lax.broadcasted_iota(jnp.int32, (rows, chunk), 1) <= row
    items = [(h, r) for h in range(0, heads, stack) for r in range(BLK // chunk)]

    def scores(h, r):
        q = [q_ref[r * chunk : (r + 1) * chunk, (h + i) * DH : (h + i + 1) * DH] for i in range(stack)]
        q = q[0] if stack == 1 else jnp.concatenate(q, axis=0)
        return dot_keys(q, keys[0 : BLK + (r + 1) * chunk, :])

    def finish(h, r, s):
        n = BLK + r * chunk
        tail = jnp.where(causal, s[:, n:], HIDDEN)
        full = s[:, :n]
        top = jnp.maximum(jnp.max(full, axis=1, keepdims=True), jnp.max(tail, axis=1, keepdims=True))
        probs = jnp.concatenate(
            [jnp.exp2((full - top) * EXPONENT).astype(BF16), jnp.exp2((tail - top) * EXPONENT).astype(BF16)], axis=1
        )
        acc = dot_values(probs, values[0 : n + chunk, :])
        out = (acc[:, :DH] / acc[:, DH:]).astype(BF16)
        for i in range(stack):
            o_ref[r * chunk : (r + 1) * chunk, (h + i) * DH : (h + i + 1) * DH] = out[i * chunk : (i + 1) * chunk]

    s = scores(*items[0])
    for n, item in enumerate(items):
        following = scores(*items[n + 1]) if n + 1 < len(items) else None
        finish(*item, s)
        s = following


def block_attention(valid, q, k, v, pieces, heads=8, chunk=128, stack=4):
    steps = GROUP // heads
    kv = pl.BlockSpec((BLK, DH), lambda g, i: (0, g))
    piece = pl.BlockSpec((2 * QUARTER, DH), lambda g, i: (0, g))
    q_spec = pl.BlockSpec((BLK, heads * DH), lambda g, i: (0, g * steps + i))
    return pl.pallas_call(
        functools.partial(block_kernel, heads, chunk, stack),
        grid=(KV_HEADS_HERE, steps),
        in_specs=[pl.BlockSpec(memory_space=pltpu.SMEM), q_spec, kv, kv, piece, piece, piece, piece],
        out_specs=q_spec,
        scratch_shapes=[pltpu.VMEM((2 * BLK, DH), BF16), pltpu.VMEM((2 * BLK, 2 * DH), BF16)],
        out_shape=jax.ShapeDtypeStruct(q.shape, BF16),
        compiler_params=pltpu.CompilerParams(vmem_limit_bytes=20 << 20),
        cost_estimate=pl.CostEstimate(flops=10**9, bytes_accessed=5 << 20, transcendentals=7 << 20),
        name="block_attention",
    )(valid, q, k, v, *pieces)


def rows_kernel(chunk, valid_ref, msg_ref, k_ref, v_ref, m1, m2, m3, *rest):
    o_ref, keys, values, sent = rest[-4:]
    g = pl.program_id(0)
    my_y = lax.axis_index("y")
    first = (lax.axis_index("z") * NXH + lax.axis_index("xh")) * NY
    valids, bases = [valid_ref[0].astype(F32)], [(first + my_y) * BLK]
    for message, step in ((m1, 3), (m2, 1), (m3, 2)):
        digits = message[BLK : BLK + 16, :].astype(F32)
        valids.append(digits[0:1, 0:1] * 256.0 + digits[8:9, 0:1])
        bases.append((first + lax.rem(my_y + step, NY)) * BLK)
    arrived = msg_ref[...].astype(F32)
    limits_in = arrived[:, 16:24, :].reshape(ROWS * GROUP, DH)
    offsets = limits_in[:, 0:1] * 256.0 + limits_in[:, 64:65]
    limits = [jnp.minimum(offsets - base.astype(F32), v) for base, v in zip(bases, valids)]
    columns = lax.broadcasted_iota(jnp.int32, (chunk, BLK), 1).astype(F32)
    keys[0:BLK, :] = k_ref[...]
    values[0:BLK, :DH] = v_ref[...]
    values[:, DH:] = jnp.ones((NY * BLK, DH), BF16)
    for i, message in enumerate((m1, m2, m3)):
        rows = slice((i + 1) * BLK, (i + 2) * BLK)
        keys[rows, :] = message[0:BLK, :]
        values[rows, :DH] = message[BLK + 16 :, :]
    queries = jnp.where(g == 0, arrived[:, :GROUP, :], arrived[:, GROUP : 2 * GROUP, :])
    queries = queries.reshape(ROWS * GROUP, DH).astype(BF16)
    starts = range(0, ROWS * GROUP, chunk)
    parts, logs = [], []
    s = dot_keys(queries[0:chunk], keys[...])
    for r in starts:
        following = dot_keys(queries[r + chunk : r + 2 * chunk], keys[...]) if r + chunk < ROWS * GROUP else None
        pieces = [
            jnp.where(columns < limits[b][r : r + chunk], s[:, b * BLK : (b + 1) * BLK], HIDDEN) for b in range(NY)
        ]
        top = jnp.max(functools.reduce(jnp.maximum, pieces), axis=1, keepdims=True)
        top = jnp.maximum(top, FLOOR)
        probs = jnp.concatenate([jnp.exp2((p - top) * EXPONENT).astype(BF16) for p in pieces], axis=1)
        acc = dot_values(probs, values[...])
        total = acc[:, DH:]
        some = total > 0.0
        parts.append(acc[:, :DH] / jnp.where(some, total, 1.0))
        logs.append(jnp.where(some, top * EXPONENT + jnp.log2(jnp.where(some, total, 1.0)), HIDDEN))
        s = following
    out = jnp.concatenate(parts, axis=0).reshape(ROWS, GROUP, DH)
    log = jnp.concatenate(logs, axis=0)
    lane = lax.broadcasted_iota(jnp.int32, (ROWS * GROUP, DH), 1) & 63
    high = log.astype(BF16).astype(F32)
    middle = (log - high).astype(BF16).astype(F32)
    low = log - high - middle
    log = jnp.where(lane == 0, high, jnp.where(lane == 1, middle, low)).reshape(ROWS, GROUP, DH)

    @pl.when(g == 0)
    def _():
        sent[:, 0:8, :] = out
        sent[:, 8:16, :] = log

    @pl.when(g == 1)
    def _():
        both = jnp.where(lane.reshape(ROWS, GROUP, DH) == lax.broadcasted_iota(jnp.int32, log.shape, 2), sent[:, 8:16, :], log)
        o_ref[...] = jnp.concatenate([sent[:, 0:8, :], out, both], axis=1).astype(BF16)


def rows_attention(valid, msg, k, v, others, after, chunk=128):
    whole = pl.BlockSpec(msg.shape, lambda g: (0, 0, 0))
    block = pl.BlockSpec((BLK, DH), lambda g: (0, g))
    other = [pl.BlockSpec((array.shape[0], DH), lambda g: (0, g)) for array in others]
    unread = [pl.BlockSpec(memory_space=pl.ANY)] * len(after)
    return pl.pallas_call(
        functools.partial(rows_kernel, chunk),
        grid=(KV_HEADS_HERE,),
        in_specs=[pl.BlockSpec(memory_space=pltpu.SMEM), whole, block, block, *other, *unread],
        out_specs=whole,
        scratch_shapes=[
            pltpu.VMEM((NY * BLK, DH), BF16),
            pltpu.VMEM((NY * BLK, 2 * DH), BF16),
            pltpu.VMEM((ROWS, 2 * GROUP, DH), F32),
        ],
        out_shape=jax.ShapeDtypeStruct(msg.shape, BF16),
        compiler_params=pltpu.CompilerParams(vmem_limit_bytes=20 << 20),
        cost_estimate=pl.CostEstimate(flops=7 * 10**9, bytes_accessed=3 << 20, transcendentals=2 << 20),
        name="rows_attention",
    )(valid, msg, k, v, *others, *after)


def merge_kernel(msg_ref, o_ref):
    arrived = msg_ref[...].astype(F32).reshape(NZ * NXH, NXL * NCORE, 24, DH)
    for h in range(NXL * NCORE):
        for g in range(KV_HEADS_HERE):
            digits = arrived[:, h, 16:24, :]
            at = 64 * g
            log = digits[:, :, at : at + 1] + digits[:, :, at + 1 : at + 2] + digits[:, :, at + 2 : at + 3]
            factor = jnp.exp2(log - jnp.max(log, axis=0, keepdims=True))
            total = jnp.sum(factor, axis=0)
            merged = jnp.sum(factor * arrived[:, h, 8 * g : 8 * g + 8, :], axis=0) / total
            for i in range(GROUP):
                at = ((h * KV_HEADS_HERE + g) * GROUP + i) * DH
                o_ref[0:1, at : at + DH] = merged[i : i + 1].astype(BF16)


def merge(msg):
    whole = pl.BlockSpec(memory_space=pltpu.VMEM)
    return pl.pallas_call(
        merge_kernel,
        in_specs=[whole],
        out_specs=whole,
        out_shape=jax.ShapeDtypeStruct((1, NXL * NCORE * KV_HEADS_HERE * GROUP * DH), BF16),
        compiler_params=pltpu.CompilerParams(vmem_limit_bytes=6 << 20),
        name="merge",
    )(msg)


def shift(n, by):
    return [(i, (i + by) % n) for i in range(n)]


def digits_of(number):
    high = number // 256
    return high.astype(BF16), (number - high * 256).astype(BF16)


def message_kernel(offset_ref, q_ref, _, o_ref, rows):
    offset = offset_ref[0]
    high, low = (offset >> 8).astype(F32), (offset & 255).astype(F32)
    lane = lax.broadcasted_iota(jnp.int32, (GROUP, DH), 1)
    limit = jnp.where(lane < 64, high, low)
    heads = KV_HEADS_HERE * GROUP
    for h in range(NXL * NCORE):
        for i in range(heads):
            at = (h * heads + i) * DH
            rows[h, i : i + 1, :] = q_ref[0:1, at : at + DH].astype(F32)
        rows[h, heads:, :] = limit
    o_ref[...] = jnp.broadcast_to(rows[...].astype(BF16)[None], o_ref.shape)


def row_message(offsets, query_rows, after):
    whole = pl.BlockSpec(memory_space=pltpu.VMEM)
    groups = NXL * NCORE
    out = pl.pallas_call(
        message_kernel,
        in_specs=[pl.BlockSpec(memory_space=pltpu.SMEM), whole, pl.BlockSpec(memory_space=pl.ANY)],
        out_specs=whole,
        scratch_shapes=[pltpu.VMEM((groups, 24, DH), F32)],
        out_shape=jax.ShapeDtypeStruct((NZ * NXH, groups, 24, DH), BF16),
        compiler_params=pltpu.CompilerParams(vmem_limit_bytes=6 << 20),
        cost_estimate=pl.CostEstimate(flops=5 * 10**10, bytes_accessed=1 << 20, transcendentals=0),
        name="row_message",
    )(offsets, query_rows, after)
    return out.reshape(PEERS, 24, DH)


def place(z, xh):
    return (z % NZ) * NXH + xh


def to_ring(array):
    return [lax.ppermute(array, "y", shift(NY, by)) for by in (1, -1, 2)]


def anchor_quarters(k, v):
    quarters = [jnp.concatenate([k[r : r + QUARTER], v[r : r + QUARTER]]) for r in range(0, BLK, QUARTER)]
    current = jnp.where(lax.axis_index(CTX) == 0, quarters[0], jnp.zeros_like(quarters[0]))
    for y in range(1, NY):
        current = current + lax.ppermute(quarters[y], CTX, [(0, y)])
    return current


def anchor_tree(current, after):
    sent = [lax.ppermute(current, ZX, [(0, place(z, 0))]) for z in (2, 4, 6)]
    current = join([current] + sent, after)
    even = (0, 2, 4, 6)
    sent = [
        lax.ppermute(current, ZX, [(place(z, 0), place(z + dz, xh)) for z in even]) for dz, xh in ((0, 1), (1, 0), (1, 1))
    ]
    return current, sent


def join_kernel(count, *refs):
    total = refs[0][...]
    for ref in refs[1:count]:
        total = total + ref[...]
    refs[-1][...] = total


def join(parts, after=()):
    whole = pl.BlockSpec(memory_space=pltpu.VMEM)
    return pl.pallas_call(
        functools.partial(join_kernel, len(parts)),
        in_specs=[whole] * len(parts) + [pl.BlockSpec(memory_space=pl.ANY)] * len(after),
        out_specs=whole,
        out_shape=jax.ShapeDtypeStruct(parts[0].shape, BF16),
        compiler_params=SMALL,
        cost_estimate=LONG,
        name="join",
    )(*parts, *after)


def on_device(ctx_query, ctx_key, ctx_value, valid, query_rows, offsets):
    high, low = digits_of(valid)
    extra = jnp.concatenate([jnp.broadcast_to(high[None], (8, 2 * DH)), jnp.broadcast_to(low[None], (8, 2 * DH))], axis=0)
    kv = jnp.concatenate([ctx_key, extra, ctx_value], axis=0)
    current = anchor_quarters(ctx_key, ctx_value)
    others = to_ring(kv)
    message = row_message(offsets, query_rows, current)
    message = lax.all_to_all(message, PLANE, 0, 0, tiled=True)
    near, sent = anchor_tree(current, others[:2])
    partial = rows_attention(valid, message, ctx_key, ctx_value, others, [near])
    current = join([near] + sent, (partial,))
    pieces = [current] + to_ring(current)
    partial = lax.all_to_all(partial, PLANE, 0, 0, tiled=True)
    block_out = block_attention(valid, ctx_query, ctx_key, ctx_value, pieces)
    return (block_out, merge(partial))


def solution(mesh):
    fine = Mesh(mesh.devices.reshape(NZ, NXH, NY, NXL, NCORE), ("z", "xh", "y", "xl", "core"))
    return jax.shard_map(
        on_device,
        mesh=fine,
        in_specs=(P(CTX, HEAD), P(CTX, HEAD), P(CTX, HEAD), P(CTX), P(CTX + HEAD, None), P(CTX + HEAD)),
        out_specs=(P(CTX, HEAD), P(CTX + HEAD, None)),
        check_vma=False,
    )
```

```python
import functools
import math

import jax
import jax.numpy as jnp
from jax import lax
from jax.experimental import pallas as pl
from jax.experimental.pallas import tpu as pltpu
from jax.sharding import Mesh, PartitionSpec as P

DH = 128
KV_HEADS_HERE = 2
GROUP = 8
BLK = 512
NZ, NXH, NY, NXL, NCORE = 8, 2, 4, 2, 2
PEERS = NZ * NXH * NXL * NCORE
ROWS = PEERS
QUARTER = BLK // NY
EXPONENT = math.log2(math.e) / math.sqrt(DH)
HIDDEN = -1e30
FLOOR = -1e29
CTX = ("z", "xh", "y")
ZX = ("z", "xh")
HEAD = ("xl", "core")
PLANE = ("z", "xh", "xl", "core")
BF16 = jnp.bfloat16
F32 = jnp.float32


SMALL = pltpu.CompilerParams(vmem_limit_bytes=6 << 20)
LONG = pl.CostEstimate(flops=5 * 10**10, bytes_accessed=1 << 20, transcendentals=0)


def dot_keys(queries, keys):
    return lax.dot_general(queries, keys, (((1,), (1,)), ((), ())), preferred_element_type=F32)


def dot_values(probs, values):
    return jnp.dot(probs, values, preferred_element_type=F32)


def block_kernel(heads, chunk, stack, valid_ref, q_ref, k_ref, v_ref, a0, a1, a2, a3, o_ref, keys, values):
    @pl.when(pl.program_id(1) == 0)
    def _():
        valid = valid_ref[0]
        seen = (lax.axis_index("z") + lax.axis_index("xh") + lax.axis_index("y")) > 0
        keep = lax.broadcasted_iota(jnp.int32, (BLK, DH), 0) < valid
        base = k_ref[0:1, :].astype(F32)
        keys[BLK:, :] = jnp.where(keep, k_ref[...].astype(F32), base).astype(BF16)
        values[BLK:, :DH] = jnp.where(keep, v_ref[...].astype(F32), 0.0).astype(BF16)
        values[BLK:, DH:] = jnp.where(keep, 1.0, 0.0).astype(BF16)
        for i, piece in enumerate((a0, a1, a2, a3)):
            rows = slice(QUARTER * i, QUARTER * (i + 1))
            keys[rows, :] = jnp.where(seen, piece[0:QUARTER, :].astype(F32), base).astype(BF16)
            values[rows, :DH] = jnp.where(seen, piece[QUARTER:, :].astype(F32), 0.0).astype(BF16)
        values[0:BLK, DH:] = jnp.where(seen, jnp.ones((BLK, DH), F32), 0.0).astype(BF16)

    rows = stack * chunk
    row = lax.broadcasted_iota(jnp.int32, (rows, chunk), 0) & (chunk - 1)
    causal = lax.broadcasted_iota(jnp.int32, (rows, chunk), 1) <= row
    items = [(h, r) for h in range(0, heads, stack) for r in range(BLK // chunk)]

    def scores(h, r):
        q = [q_ref[r * chunk : (r + 1) * chunk, (h + i) * DH : (h + i + 1) * DH] for i in range(stack)]
        q = q[0] if stack == 1 else jnp.concatenate(q, axis=0)
        return dot_keys(q, keys[0 : BLK + (r + 1) * chunk, :])

    def finish(h, r, s):
        n = BLK + r * chunk
        tail = jnp.where(causal, s[:, n:], HIDDEN)
        full = s[:, :n]
        top = jnp.maximum(jnp.max(full, axis=1, keepdims=True), jnp.max(tail, axis=1, keepdims=True))
        probs = jnp.concatenate(
            [jnp.exp2((full - top) * EXPONENT).astype(BF16), jnp.exp2((tail - top) * EXPONENT).astype(BF16)], axis=1
        )
        acc = dot_values(probs, values[0 : n + chunk, :])
        out = (acc[:, :DH] / acc[:, DH:]).astype(BF16)
        for i in range(stack):
            o_ref[r * chunk : (r + 1) * chunk, (h + i) * DH : (h + i + 1) * DH] = out[i * chunk : (i + 1) * chunk]

    s = scores(*items[0])
    for n, item in enumerate(items):
        following = scores(*items[n + 1]) if n + 1 < len(items) else None
        finish(*item, s)
        s = following


def block_attention(valid, q, k, v, pieces, heads=8, chunk=128, stack=4):
    steps = GROUP // heads
    kv = pl.BlockSpec((BLK, DH), lambda g, i: (0, g))
    piece = pl.BlockSpec((2 * QUARTER, DH), lambda g, i: (0, g))
    q_spec = pl.BlockSpec((BLK, heads * DH), lambda g, i: (0, g * steps + i))
    return pl.pallas_call(
        functools.partial(block_kernel, heads, chunk, stack),
        grid=(KV_HEADS_HERE, steps),
        in_specs=[pl.BlockSpec(memory_space=pltpu.SMEM), q_spec, kv, kv, piece, piece, piece, piece],
        out_specs=q_spec,
        scratch_shapes=[pltpu.VMEM((2 * BLK, DH), BF16), pltpu.VMEM((2 * BLK, 2 * DH), BF16)],
        out_shape=jax.ShapeDtypeStruct(q.shape, BF16),
        compiler_params=pltpu.CompilerParams(vmem_limit_bytes=20 << 20),
        cost_estimate=pl.CostEstimate(flops=10**9, bytes_accessed=5 << 20, transcendentals=7 << 20),
        name="block_attention",
    )(valid, q, k, v, *pieces)


def rows_kernel(chunk, valid_ref, msg_ref, k_ref, v_ref, m1, m2, m3, *rest):
    o_ref, keys, values, sent = rest[-4:]
    g = pl.program_id(0)
    my_y = lax.axis_index("y")
    first = (lax.axis_index("z") * NXH + lax.axis_index("xh")) * NY
    valids, bases = [valid_ref[0].astype(F32)], [(first + my_y) * BLK]
    for message, step in ((m1, 3), (m2, 1), (m3, 2)):
        digits = message[BLK : BLK + 16, :].astype(F32)
        valids.append(digits[0:1, 0:1] * 256.0 + digits[8:9, 0:1])
        bases.append((first + lax.rem(my_y + step, NY)) * BLK)
    arrived = msg_ref[...].astype(F32)
    limits_in = arrived[:, 16:24, :].reshape(ROWS * GROUP, DH)
    offsets = limits_in[:, 0:1] * 256.0 + limits_in[:, 64:65]
    limits = [jnp.minimum(offsets - base.astype(F32), v) for base, v in zip(bases, valids)]
    columns = lax.broadcasted_iota(jnp.int32, (chunk, BLK), 1).astype(F32)
    keys[0:BLK, :] = k_ref[...]
    values[0:BLK, :DH] = v_ref[...]
    values[:, DH:] = jnp.ones((NY * BLK, DH), BF16)
    for i, message in enumerate((m1, m2, m3)):
        rows = slice((i + 1) * BLK, (i + 2) * BLK)
        keys[rows, :] = message[0:BLK, :]
        values[rows, :DH] = message[BLK + 16 :, :]
    queries = jnp.where(g == 0, arrived[:, :GROUP, :], arrived[:, GROUP : 2 * GROUP, :])
    queries = queries.reshape(ROWS * GROUP, DH).astype(BF16)
    starts = range(0, ROWS * GROUP, chunk)
    parts, logs = [], []
    s = dot_keys(queries[0:chunk], keys[...])
    for r in starts:
        following = dot_keys(queries[r + chunk : r + 2 * chunk], keys[...]) if r + chunk < ROWS * GROUP else None
        pieces = [
            jnp.where(columns < limits[b][r : r + chunk], s[:, b * BLK : (b + 1) * BLK], HIDDEN) for b in range(NY)
        ]
        top = jnp.max(functools.reduce(jnp.maximum, pieces), axis=1, keepdims=True)
        top = jnp.maximum(top, FLOOR)
        probs = jnp.concatenate([jnp.exp2((p - top) * EXPONENT).astype(BF16) for p in pieces], axis=1)
        acc = dot_values(probs, values[...])
        total = acc[:, DH:]
        some = total > 0.0
        parts.append(acc[:, :DH] / jnp.where(some, total, 1.0))
        logs.append(jnp.where(some, top * EXPONENT + jnp.log2(jnp.where(some, total, 1.0)), HIDDEN))
        s = following
    out = jnp.concatenate(parts, axis=0).reshape(ROWS, GROUP, DH)
    log = jnp.concatenate(logs, axis=0)
    lane = lax.broadcasted_iota(jnp.int32, (ROWS * GROUP, DH), 1) & 63
    high = log.astype(BF16).astype(F32)
    middle = (log - high).astype(BF16).astype(F32)
    low = log - high - middle
    log = jnp.where(lane == 0, high, jnp.where(lane == 1, middle, low)).reshape(ROWS, GROUP, DH)

    @pl.when(g == 0)
    def _():
        sent[:, 0:8, :] = out
        sent[:, 8:16, :] = log

    @pl.when(g == 1)
    def _():
        both = jnp.where(lane.reshape(ROWS, GROUP, DH) == lax.broadcasted_iota(jnp.int32, log.shape, 2), sent[:, 8:16, :], log)
        o_ref[...] = jnp.concatenate([sent[:, 0:8, :], out, both], axis=1).astype(BF16)


def rows_attention(valid, msg, k, v, others, after, chunk=128):
    whole = pl.BlockSpec(msg.shape, lambda g: (0, 0, 0))
    block = pl.BlockSpec((BLK, DH), lambda g: (0, g))
    other = [pl.BlockSpec((array.shape[0], DH), lambda g: (0, g)) for array in others]
    unread = [pl.BlockSpec(memory_space=pl.ANY)] * len(after)
    return pl.pallas_call(
        functools.partial(rows_kernel, chunk),
        grid=(KV_HEADS_HERE,),
        in_specs=[pl.BlockSpec(memory_space=pltpu.SMEM), whole, block, block, *other, *unread],
        out_specs=whole,
        scratch_shapes=[
            pltpu.VMEM((NY * BLK, DH), BF16),
            pltpu.VMEM((NY * BLK, 2 * DH), BF16),
            pltpu.VMEM((ROWS, 2 * GROUP, DH), F32),
        ],
        out_shape=jax.ShapeDtypeStruct(msg.shape, BF16),
        compiler_params=pltpu.CompilerParams(vmem_limit_bytes=20 << 20),
        cost_estimate=pl.CostEstimate(flops=7 * 10**9, bytes_accessed=3 << 20, transcendentals=2 << 20),
        name="rows_attention",
    )(valid, msg, k, v, *others, *after)


def merge_kernel(msg_ref, o_ref):
    arrived = msg_ref[...].astype(F32).reshape(NZ * NXH, NXL * NCORE, 24, DH)
    for h in range(NXL * NCORE):
        for g in range(KV_HEADS_HERE):
            digits = arrived[:, h, 16:24, :]
            at = 64 * g
            log = digits[:, :, at : at + 1] + digits[:, :, at + 1 : at + 2] + digits[:, :, at + 2 : at + 3]
            factor = jnp.exp2(log - jnp.max(log, axis=0, keepdims=True))
            total = jnp.sum(factor, axis=0)
            merged = jnp.sum(factor * arrived[:, h, 8 * g : 8 * g + 8, :], axis=0) / total
            for i in range(GROUP):
                at = ((h * KV_HEADS_HERE + g) * GROUP + i) * DH
                o_ref[0:1, at : at + DH] = merged[i : i + 1].astype(BF16)


def merge(msg):
    whole = pl.BlockSpec(memory_space=pltpu.VMEM)
    return pl.pallas_call(
        merge_kernel,
        in_specs=[whole],
        out_specs=whole,
        out_shape=jax.ShapeDtypeStruct((1, NXL * NCORE * KV_HEADS_HERE * GROUP * DH), BF16),
        compiler_params=pltpu.CompilerParams(vmem_limit_bytes=6 << 20),
        name="merge",
    )(msg)


def shift(n, by):
    return [(i, (i + by) % n) for i in range(n)]


def digits_of(number):
    high = number // 256
    return high.astype(BF16), (number - high * 256).astype(BF16)


def message_kernel(offset_ref, q_ref, _, o_ref, rows):
    offset = offset_ref[0]
    high, low = (offset >> 8).astype(F32), (offset & 255).astype(F32)
    lane = lax.broadcasted_iota(jnp.int32, (GROUP, DH), 1)
    limit = jnp.where(lane < 64, high, low)
    heads = KV_HEADS_HERE * GROUP
    for h in range(NXL * NCORE):
        for i in range(heads):
            at = (h * heads + i) * DH
            rows[h, i : i + 1, :] = q_ref[0:1, at : at + DH].astype(F32)
        rows[h, heads:, :] = limit
    o_ref[...] = jnp.broadcast_to(rows[...].astype(BF16)[None], o_ref.shape)


def row_message(offsets, query_rows, after):
    whole = pl.BlockSpec(memory_space=pltpu.VMEM)
    groups = NXL * NCORE
    out = pl.pallas_call(
        message_kernel,
        in_specs=[pl.BlockSpec(memory_space=pltpu.SMEM), whole, pl.BlockSpec(memory_space=pl.ANY)],
        out_specs=whole,
        scratch_shapes=[pltpu.VMEM((groups, 24, DH), F32)],
        out_shape=jax.ShapeDtypeStruct((NZ * NXH, groups, 24, DH), BF16),
        compiler_params=pltpu.CompilerParams(vmem_limit_bytes=6 << 20),
        cost_estimate=pl.CostEstimate(flops=5 * 10**10, bytes_accessed=1 << 20, transcendentals=0),
        name="row_message",
    )(offsets, query_rows, after)
    return out.reshape(PEERS, 24, DH)


def place(z, xh):
    return (z % NZ) * NXH + xh


def to_ring(array):
    return [lax.ppermute(array, "y", shift(NY, by)) for by in (1, -1, 2)]


def anchor_quarters(k, v):
    quarters = [jnp.concatenate([k[r : r + QUARTER], v[r : r + QUARTER]]) for r in range(0, BLK, QUARTER)]
    current = jnp.where(lax.axis_index(CTX) == 0, quarters[0], jnp.zeros_like(quarters[0]))
    for y in (1, 3, 2):
        current = current + lax.ppermute(quarters[y], CTX, [(0, y)])
    return current


def anchor_tree(current, after):
    sent = [lax.ppermute(current, ZX, [(0, place(z, 0))]) for z in (2, 6, 4)]
    current = join([current] + sent, after)
    even = (0, 2, 4, 6)
    sent = [
        lax.ppermute(current, ZX, [(place(z, 0), place(z + dz, xh)) for z in even]) for dz, xh in ((0, 1), (1, 0), (1, 1))
    ]
    return current, sent


def join_kernel(count, *refs):
    total = refs[0][...]
    for ref in refs[1:count]:
        total = total + ref[...]
    refs[-1][...] = total


def join(parts, after=()):
    whole = pl.BlockSpec(memory_space=pltpu.VMEM)
    return pl.pallas_call(
        functools.partial(join_kernel, len(parts)),
        in_specs=[whole] * len(parts) + [pl.BlockSpec(memory_space=pl.ANY)] * len(after),
        out_specs=whole,
        out_shape=jax.ShapeDtypeStruct(parts[0].shape, BF16),
        compiler_params=SMALL,
        cost_estimate=LONG,
        name="join",
    )(*parts, *after)


def on_device(ctx_query, ctx_key, ctx_value, valid, query_rows, offsets):
    high, low = digits_of(valid)
    extra = jnp.concatenate([jnp.broadcast_to(high[None], (8, 2 * DH)), jnp.broadcast_to(low[None], (8, 2 * DH))], axis=0)
    kv = jnp.concatenate([ctx_key, extra, ctx_value], axis=0)
    current = anchor_quarters(ctx_key, ctx_value)
    others = to_ring(kv)
    message = row_message(offsets, query_rows, current)
    message = lax.all_to_all(message, PLANE, 0, 0, tiled=True)
    near, sent = anchor_tree(current, others[:2])
    partial = rows_attention(valid, message, ctx_key, ctx_value, others, [near])
    current = join([near] + sent, (partial,))
    pieces = [current] + to_ring(current)
    partial = lax.all_to_all(partial, PLANE, 0, 0, tiled=True)
    block_out = block_attention(valid, ctx_query, ctx_key, ctx_value, pieces)
    return (block_out, merge(partial))


def solution(mesh):
    fine = Mesh(mesh.devices.reshape(NZ, NXH, NY, NXL, NCORE), ("z", "xh", "y", "xl", "core"))
    return jax.shard_map(
        on_device,
        mesh=fine,
        in_specs=(P(CTX, HEAD), P(CTX, HEAD), P(CTX, HEAD), P(CTX), P(CTX + HEAD, None), P(CTX + HEAD)),
        out_specs=(P(CTX, HEAD), P(CTX + HEAD, None)),
        check_vma=False,
    )
```
